512 devices in a mesh: dom: 128 (over x, z, core), batch: 4 (over y).
Axes of the slice: x: 4, y: 4, z: 16, core: 2. Of those that a mesh axis runs over, the one named last changes fastest.
Arguments:
- features: bfloat16 [128, 1024, 256], P('dom', 'batch'), may hold values from -6 to 6
- initial: bfloat16 [128, 1024, 256], P('dom', 'batch'), may hold values from -6 to 6
- grad_output: bfloat16 [128, 1024, 256], P('dom', 'batch'), may hold values from -6 to 6
- weight: bfloat16 [256, 256], replicated, may hold values from -0.375 to 0.375
- history: bfloat16 [128, 4096, 256], P('dom'), may hold values from -6 to 6
- halo_table: int32 [128, 4, 128, 8], P('dom', 'batch'), may hold values from -1 to 4095, as said below
- tile_cols: int32 [128, 4, 2, 8], P('dom', 'batch'), may hold values from 0 to 9, as said below
- tile_vals: bfloat16 [128, 4, 2, 8, 128, 128], P('dom', 'batch'), may hold values from -0.1875 to 0.1875
- batch_ids: int32 [128, 4, 256], P('dom'), may hold values from -1 to 4095, as said below
Outputs:
- new_history: bfloat16 [128, 4096, 256], P('dom')
- grad_features: bfloat16 [128, 1024, 256], P('dom', 'batch')
- grad_weight: float32 [256, 256], replicated
The draws below stay inside these ranges and needn't reach their ends.
Inputs may be any that keep to these rules, and one draw needn't show every extreme that they name: `halo_table`: every device's table holds 8 live slots for its own partition and its two neighbours modulo 128; for every other owner at most 2 live slots, exactly 2 for the partition two above its own modulo 128; live slots of an owner come first. `tile_cols`: within each row block the 8 column blocks are distinct, and the first is the row block's own local block. `batch_ids`: live slots come first; live rows are distinct over all batch indices of one partition; in each partition one device has all slots live.
All inputs are finite; a program needn't handle non-finite values.
Results may differ from the reference program's by a relative error of at most 0.011.
Values may be sent and summed in bfloat16 or wider, within the bound.
A program may use at most 64 MiB of HBM per device.

```python
import math
import jax
import jax.numpy as jnp
from jax import lax

H = 256
TILE = 128
BATCH_DEV = 256
HIST_ROWS = 4096
K = 8
CAP = 8
FAR = 2
RB = 2
CB = 10
PART_ROWS = 1024
N_DOM = 128
N_BATCH = 4


def draw_halo_table(key, part):
    key = jax.random.fold_in(key, 11)
    count_key, row_key = jax.random.split(key)
    shape = (N_DOM, N_BATCH, N_DOM)
    counts = jax.random.randint(count_key, shape, 0, FAR + 1)
    dom_index = jnp.arange(N_DOM)[:, None, None]
    owner = jnp.arange(N_DOM)[None, None, :]
    offset = (owner - dom_index) % N_DOM
    counts = jnp.where(offset == 2, FAR, counts)
    nearby = (offset == 0) | (offset == 1) | (offset == N_DOM - 1)
    counts = jnp.where(nearby, CAP, counts)
    rows_drawn = jax.random.randint(row_key, shape + (CAP,), 0, HIST_ROWS)
    slot = jnp.arange(CAP)
    return jnp.where(slot < counts[..., None], rows_drawn, -1).astype(jnp.int32)


def draw_tile_cols(key, part):
    key = jax.random.fold_in(key, 12)
    shape = (N_DOM, N_BATCH, RB, CB)
    scores = jax.random.randint(key, shape, 0, 1 << 19) * CB + jnp.arange(CB)
    own_block = jnp.arange(RB)[:, None] == jnp.arange(CB)[None, :]
    scores = jnp.where(own_block, -1, scores)
    order = jnp.argsort(scores, axis=-1, stable=True)
    return order[..., :K].astype(jnp.int32)


def draw_batch_ids(key, part):
    key = jax.random.fold_in(key, 13)
    order_key, count_key = jax.random.split(key)
    scores = jax.random.randint(order_key, (N_DOM, HIST_ROWS), 0, 1 << 10) * HIST_ROWS + jnp.arange(HIST_ROWS)
    chosen = jnp.argsort(scores, axis=-1, stable=True)[:, :N_BATCH * BATCH_DEV].reshape(N_DOM, N_BATCH, BATCH_DEV)
    counts = jax.random.randint(count_key, (N_DOM, N_BATCH), BATCH_DEV // 4, BATCH_DEV + 1)
    full = jnp.arange(N_BATCH)[None, :] == jnp.arange(N_DOM)[:, None] % N_BATCH
    counts = jnp.where(full, BATCH_DEV, counts)
    slot = jnp.arange(BATCH_DEV)
    return jnp.where(slot < counts[..., None], chosen, -1).astype(jnp.int32)


def block_scale(rng, extent, cuts, least, high):
    gain, own = 1.0, jax.random.fold_in(rng, 6)
    for dim, parts in cuts:
        draws = jnp.exp(jax.random.uniform(jax.random.fold_in(own, dim), (parts,), jnp.float32, least / len(cuts), high / len(cuts)))
        gain = gain * jnp.repeat(draws, extent[dim] // parts).reshape([-1 if axis == dim else 1 for axis in range(len(extent))])
    return gain


def centred(stream_key, dims, width, reach, cuts=(), kind=jnp.bfloat16):
    drawn = jax.random.normal(stream_key, dims, jnp.float32) * width
    if len(cuts) > 0:
        drawn = block_scale(stream_key, dims, cuts, -0.22, 0.18) * drawn
    return jnp.clip(drawn, min=-reach, max=reach).astype(kind)


def setup_inputs(seed: int = 0) -> dict:
    streams_of = jax.random.split(jax.random.key(seed), 10)
    features = centred(streams_of[0], (N_DOM, PART_ROWS, H), 1.0, 6.0, ((0, 128), (1, 4)))
    initial = centred(streams_of[1], (N_DOM, PART_ROWS, H), 1.0, 6.0, ((0, 128), (1, 4)))
    grad_output = centred(streams_of[2], (N_DOM, PART_ROWS, H), 1.0, 6.0, ((0, 128), (1, 4)))
    weight = centred(streams_of[3], (H, H), H ** -0.5, 0.375)
    history = centred(streams_of[4], (N_DOM, HIST_ROWS, H), 1.0, 6.0, ((0, 128),))
    halo_table = draw_halo_table(jax.random.fold_in(streams_of[9], 71), 0)
    tile_cols = draw_tile_cols(jax.random.fold_in(streams_of[9], 71), 0)
    tile_vals = centred(streams_of[7], (N_DOM, N_BATCH, RB, K, TILE, TILE), (K * TILE) ** -0.5, 0.1875, ((0, 128), (1, 4)))
    batch_ids = draw_batch_ids(jax.random.fold_in(streams_of[9], 71), 0)
    return {"features": features, "initial": initial, "grad_output": grad_output, "weight": weight, "history": history, "halo_table": halo_table, "tile_cols": tile_cols, "tile_vals": tile_vals, "batch_ids": batch_ids}


ALPHA_MIX = 0.1
BETA_MIX = math.log(1.5)


def layer_pass(features, initial, grad_output, weight, halo_rows, tile_cols, tile_vals, own_ids):
    row_count = features.shape[0]
    feature = features.shape[1]
    tile_size = tile_vals.shape[-1]
    row_blocks = row_count // tile_size
    is_live = (own_ids >= 0)[:, None]
    masked = jnp.where(is_live, features, jnp.zeros_like(features))
    blocks = jnp.concatenate([masked.reshape(row_blocks, tile_size, feature), halo_rows.reshape(-1, tile_size, feature)], axis=0)
    picked = jnp.take(blocks, tile_cols, axis=0)
    aggregate = jnp.einsum("rkij,rkjh->rih", tile_vals.astype(jnp.float32), picked.astype(jnp.float32)).reshape(row_count, feature)
    support = (1.0 - ALPHA_MIX) * aggregate + ALPHA_MIX * initial.astype(jnp.float32)
    support_low = support.astype(jnp.bfloat16)
    pre_act = (1.0 - BETA_MIX) * support + BETA_MIX * jnp.dot(support_low, weight, preferred_element_type=jnp.float32)
    outputs = jax.nn.silu(pre_act).astype(jnp.bfloat16)
    sigmoid_z = jax.nn.sigmoid(pre_act)
    slope = grad_output.astype(jnp.float32) * sigmoid_z * (1.0 + pre_act * (1.0 - sigmoid_z))
    grad_pre = jnp.where(is_live, slope, jnp.zeros_like(slope))
    grad_low = grad_pre.astype(jnp.bfloat16)
    grad_w = BETA_MIX * jnp.dot(support_low.T, grad_low, preferred_element_type=jnp.float32)
    grad_sup = (1.0 - BETA_MIX) * grad_pre + BETA_MIX * jnp.dot(grad_low, weight.T, preferred_element_type=jnp.float32)
    grad_agg = ((1.0 - ALPHA_MIX) * grad_sup).astype(jnp.bfloat16)
    spread = jnp.einsum("rkij,rih->rkjh", tile_vals.astype(jnp.float32), grad_agg.reshape(row_blocks, tile_size, feature).astype(jnp.float32))
    onehot = (tile_cols[:, :, None] == jnp.arange(row_blocks, dtype=jnp.int32)[None, None, :]).astype(jnp.float32)
    grad_x = jnp.einsum("rkc,rkjh->cjh", onehot, spread).reshape(row_count, feature)
    grad_x = jnp.where(is_live, grad_x, jnp.zeros_like(grad_x)).astype(jnp.bfloat16)
    return outputs, grad_x, grad_w


def reference(features, initial, grad_output, weight, history, halo_table, tile_cols, tile_vals, batch_ids):
    doms = history.shape[0]
    hist_rows = history.shape[1]
    feature = history.shape[2]
    devices = doms * N_BATCH
    per_dev = features.shape[1] // N_BATCH

    def one_device(index):
        dom_index = index // N_BATCH
        batch_index = index % N_BATCH
        requests = halo_table[dom_index, batch_index]
        owners = jnp.arange(doms, dtype=jnp.int32)[:, None]
        fetched = history[owners, jnp.clip(requests, 0, hist_rows - 1)]
        fetched = jnp.where((requests >= 0)[:, :, None], fetched, jnp.zeros_like(fetched)).reshape(-1, feature)
        start = (batch_index * per_dev).astype(jnp.int32)
        return layer_pass(
            lax.dynamic_slice_in_dim(features[dom_index], start, per_dev, 0),
            lax.dynamic_slice_in_dim(initial[dom_index], start, per_dev, 0),
            lax.dynamic_slice_in_dim(grad_output[dom_index], start, per_dev, 0),
            weight, fetched, tile_cols[dom_index, batch_index], tile_vals[dom_index, batch_index],
            batch_ids[dom_index, batch_index])

    outputs, grad_x, grad_w = lax.map(one_device, jnp.arange(devices, dtype=jnp.int32))
    grad_weight = jnp.sum(grad_w, axis=0) / devices
    owner_base = (jnp.arange(devices, dtype=jnp.int32) // N_BATCH) * hist_rows
    slot_ids = batch_ids.reshape(devices, per_dev)
    target = jnp.where(slot_ids >= 0, slot_ids + owner_base[:, None], doms * hist_rows).astype(jnp.int32)
    flat = history.reshape(doms * hist_rows, feature).at[target.reshape(-1)].set(outputs.reshape(-1, feature), mode="drop")
    new_history = flat.reshape(history.shape)
    return new_history, grad_x.reshape(features.shape), grad_weight
```

```python
import math

import jax
import jax.numpy as jnp
from jax import lax
from jax.experimental import pallas as pl
from jax.experimental.pallas import tpu as pltpu
from jax.sharding import PartitionSpec as P

ALPHA_MIX = 0.1
BETA_MIX = math.log(1.5)
X, Z, C, Y = 4, 16, 2, 4
N_DOM = X * Z * C
GROUP = X * Y * C
H = 256
TILE = 128
ROWS = 256
HIST = 4096
CAP = 8
K = 8
NB = 2 + N_DOM * CAP // TILE
PART = Y * ROWS
BASE = 8192
CHUNK = 512
BF = jnp.bfloat16
F32 = jnp.float32
I32 = jnp.int32


def coords():
    d = lax.axis_index("dom")
    return lax.div(d, Z * C), lax.rem(lax.div(d, C), Z), lax.rem(d, C), lax.axis_index("batch")


def dom_of(x, z, c):
    return (x * Z + z) * C + c


def each_dom_peer(fn):
    x, z, c, _ = coords()

    def plane(zz, own):
        for dx in (2, 1, 3, 0):
            for dc in (1, 0):
                if not (own and dx == 0 and dc == 0):
                    fn(dom_of(lax.rem(x + dx, X), zz, lax.rem(c + dc, C)))

    def body(k, carry):
        odd, half = lax.rem(k, 2), lax.div(k, 2)
        plane(lax.rem(z + Z // 2 + half * (1 - 2 * odd) - odd, Z), False)
        return carry

    lax.fori_loop(0, Z - 1, body, 0)
    plane(z, True)


def group_peers(skip_same_batch):
    x, z, c, b = coords()
    out = []
    for dx in (2, 1, 3, 0):
        for dy in (2, 1, 3, 0):
            for dc in (1, 0):
                if (dx, dy, dc) == (0, 0, 0) or (skip_same_batch and dy == 0):
                    continue
                qx, qy, qc = lax.rem(x + dx, X), lax.rem(b + dy, Y), lax.rem(c + dc, C)
                out.append(((qx * Y + qy) * C + qc, {"dom": dom_of(qx, z, qc), "batch": qy}))
    return out


def z_peers():
    x, z, c, _ = coords()
    return [{"dom": dom_of(x, lax.rem(z + i, Z), c)} for i in (8, 7, 9, 6, 10, 5, 11, 4, 12, 3, 13, 2, 14, 1, 15)]


def remote(src, dst, send, recv, device):
    return pltpu.make_async_remote_copy(src_ref=src, dst_ref=dst, send_sem=send, recv_sem=recv, device_id=device)


def wait_bytes(like, sem):
    pltpu.make_async_copy(like, like, sem).wait()


def iota(shape, dim):
    return lax.broadcasted_iota(I32, shape, dim)


def ones_where(mask):
    return jnp.where(mask, 1.0, 0.0).astype(BF)


def mm(a, b, dims=((1,), (0,))):
    return lax.dot_general(a, b, (dims, ((), ())), preferred_element_type=F32)


def kernel(
    tab_h, ids_h, cols_h, hist_h, feat_h, init_h, gout_h, w_h, tiles_h,
    nh_o, gx_o, gw_o,
    tab, ids, cols, hist, feat, init, gout, w, tiles,
    req, wreq, ntab, sbuf, rbuf, nsend, nrow, perm, e_lo, e_hi, e_near, place, blocks, live,
    outs, gsend, grecv, zsend, zrecv, asend, arecv,
    in_sem, req_s, req_r, nreq_s, nreq_r, row_s, row_r, nrow_s, nrow_r, rs_s, rs_r, z_s, z_r, ag_s, ag_r, y_s, y_r, out_sem,
):
    x, z, c, b = coords()
    me = lax.axis_index("dom")
    pairs = [
        (tab_h, tab), (ids_h, ids), (cols_h, cols), (hist_h, hist), (feat_h, feat),
        (init_h, init), (gout_h, gout), (w_h, w), (tiles_h, tiles),
    ]
    loads = [pltpu.make_async_copy(src, dst, in_sem.at[i]) for i, (src, dst) in enumerate(pairs)]
    for load in loads:
        load.start()

    barrier = pltpu.get_barrier_semaphore()
    each_dom_peer(lambda p: pl.semaphore_signal(barrier, inc=1, device_id={"dom": p}))
    others = group_peers(True)
    for _, device in others:
        pl.semaphore_signal(barrier, inc=1, device_id=device)

    loads[0].wait()
    req[...] = (tab[0:1, :] + 1) * BASE + (tab[1:2, :] + 1)
    wreq[pl.ds(me, 1)] = jnp.zeros((1, 1, N_DOM), I32)
    right, left = lax.rem(me + 1, N_DOM), lax.rem(me + N_DOM - 1, N_DOM)
    pl.semaphore_wait(barrier, N_DOM - 1 + len(others))
    near_req = [remote(tab, ntab.at[i], nreq_s.at[i], nreq_r.at[i], {"dom": p}) for i, p in enumerate((right, left))]
    for copy in near_req:
        copy.start()
    each_dom_peer(lambda p: remote(req, wreq.at[me], req_s, req_r, {"dom": p}).start())

    loads[1].wait()

    def place_chunk(i, carry):
        rows = iota((CHUNK, ROWS), 0) + i * CHUNK
        for q in range(Y):
            place[pl.ds(pl.multiple_of(i * CHUNK, CHUNK), CHUNK), pl.ds(q * ROWS, ROWS)] = ones_where(rows == ids[q : q + 1, :])
        return carry

    lax.fori_loop(0, HIST // CHUNK, place_chunk, 0)
    r4 = iota((4 * N_DOM, 2 * N_DOM), 0)
    pick = lax.rem(r4, 4) // 2 * N_DOM + r4 // 4 == iota((4 * N_DOM, 2 * N_DOM), 1)
    perm[:, 0 : 2 * N_DOM] = ones_where(pick & (lax.rem(r4, 2) == 0))
    perm[:, 2 * N_DOM :] = ones_where(pick & (lax.rem(r4, 2) == 1))
    loads[3].wait()

    wait_bytes(wreq.at[pl.ds(0, N_DOM - 1)], req_r)
    for copy in near_req:
        copy.wait_recv()

    lane_me = iota((1, N_DOM), 1) == me

    def column(v):
        return jnp.sum(jnp.where(lane_me, v.astype(F32), 0.0), axis=1, keepdims=True)

    asked = wreq[...].reshape(N_DOM, N_DOM)
    wanted = jnp.concatenate(
        [
            column(lax.shift_right_logical(asked, 13) - 1),
            column(jnp.bitwise_and(asked, BASE - 1) - 1),
            column(tab[...]),
            column(ntab[0]),
            column(ntab[1]),
            jnp.full((8, 1), -1.0, F32),
        ],
        axis=0,
    ).astype(I32)
    n_ask = 2 * N_DOM + 32
    got = jnp.zeros((n_ask, H), F32)
    for i in range(HIST // CHUNK):
        hot = ones_where(wanted == iota((n_ask, CHUNK), 1) + i * CHUNK)
        got = got + mm(hot, hist[pl.ds(i * CHUNK, CHUNK), :])
    n0 = 2 * N_DOM
    nsend[0] = got[n0 + 16 : n0 + 24, :].astype(BF)
    nsend[1] = got[n0 + 8 : n0 + 16, :].astype(BF)
    near_row = [remote(nsend.at[i], nrow.at[i], nrow_s.at[i], nrow_r.at[i], {"dom": p}) for i, p in enumerate((right, left))]
    for copy in near_row:
        copy.start()
    far = got[0:n0, :].astype(BF)
    halves = jnp.concatenate([far[:, 0:TILE], far[:, TILE:]], axis=0)
    sbuf[...] = mm(perm[...], halves).astype(BF).reshape(N_DOM, 4, TILE)
    rbuf[pl.ds(me, 1)] = jnp.zeros((1, 4, TILE), BF)
    each_dom_peer(lambda p: remote(sbuf.at[p], rbuf.at[me], row_s, row_r, {"dom": p}).start())

    own_rows = got[n0 : n0 + 8, :]
    shape = (N_DOM * CAP, 4 * N_DOM)
    p_row, p_col = iota(shape, 0), iota(shape, 1)
    slot = lax.rem(p_row, CAP)
    spot = jnp.where(slot < 2, p_row // CAP * 4 + slot * 2, -8)
    e_lo[...] = ones_where(p_col == spot)
    e_hi[...] = ones_where(p_col == spot + 1)
    shape = (N_DOM * CAP, 32)
    p_row, p_col = iota(shape, 0), iota(shape, 1)
    who, slot = p_col // 8, lax.rem(p_col, 8)
    owner = jnp.where(who == 0, me, jnp.where(who == 1, left, right))
    e_near[...] = ones_where((p_row == owner * CAP + slot) & (who < 3) & ((who == 0) | (slot >= 2)))
    mine = jnp.sum(jnp.where(iota((Y, ROWS), 0) == b, (ids[...] >= 0).astype(F32), 0.0), axis=0, keepdims=True)
    live_col = jnp.sum(jnp.where(iota((ROWS, ROWS), 0) == iota((ROWS, ROWS), 1), mine, 0.0), axis=1, keepdims=True)
    live[...] = jnp.broadcast_to(live_col, (ROWS, H))
    loads[4].wait()
    masked = jnp.where(live[...] > 0, feat[...].astype(F32), 0.0).astype(BF)
    blocks[0:2] = masked.reshape(2, TILE, H)

    def clear_chunk(i, carry):
        rows = pl.ds(pl.multiple_of(i * CHUNK, CHUNK), CHUNK)
        hit = jnp.max(place[rows, :].astype(F32), axis=1, keepdims=True)
        hist[rows, :] = jnp.where(hit > 0, 0.0, hist[rows, :].astype(F32)).astype(BF)
        return carry

    lax.fori_loop(0, HIST // CHUNK, clear_chunk, 0)
    for load in (loads[2], *loads[5:]):
        load.wait()

    for copy in near_row:
        copy.wait_recv()
    wait_bytes(rbuf.at[pl.ds(0, N_DOM - 1)], row_r)

    near = jnp.concatenate([own_rows, nrow[0].astype(F32), nrow[1].astype(F32), jnp.zeros((8, H), F32)], axis=0).astype(BF)
    near = mm(e_near[...], near)
    came = rbuf[...].reshape(4 * N_DOM, TILE)
    blocks[2:NB, :, 0:TILE] = (mm(e_lo[...], came) + near[:, 0:TILE]).astype(BF).reshape(NB - 2, TILE, TILE)
    blocks[2:NB, :, TILE:] = (mm(e_hi[...], came) + near[:, TILE:]).astype(BF).reshape(NB - 2, TILE, TILE)

    agg = []
    for r in range(2):
        total = None
        for k in range(0, K, 2):
            lhs = jnp.concatenate([tiles[r, k], tiles[r, k + 1]], axis=1)
            rhs = jnp.concatenate([blocks[cols[r, k]], blocks[cols[r, k + 1]]], axis=0)
            term = mm(lhs, rhs)
            total = term if total is None else total + term
        agg.append(total)
    support = (1.0 - ALPHA_MIX) * jnp.concatenate(agg, axis=0) + ALPHA_MIX * init[...].astype(F32)
    support_low = support.astype(BF)
    pre_act = (1.0 - BETA_MIX) * support + BETA_MIX * mm(support_low, w[...])
    sig = jax.nn.sigmoid(pre_act)
    slope = gout[...].astype(F32) * sig * (1.0 + pre_act * (1.0 - sig))
    grad_pre = jnp.where(live[...] > 0, slope, 0.0)
    grad_low = grad_pre.astype(BF)
    grad_w = mm(support_low, grad_low, ((0,), (0,)))

    gsend[...] = grad_w.astype(BF).reshape(GROUP, H // GROUP, H)
    slice_me = (x * Y + b) * C + c
    peers = group_peers(False)
    for slot_q, device in peers:
        remote(gsend.at[slot_q], grecv.at[slice_me], rs_s, rs_r, device).start()
    outs[pl.ds(b, 1)] = (pre_act * sig).astype(BF).reshape(1, ROWS, H)
    y_right, y_left = {"batch": lax.rem(b + 1, Y)}, {"batch": lax.rem(b + Y - 1, Y)}
    ring = [remote(outs.at[b], outs.at[b], y_s.at[i], y_r.at[i], p) for i, p in enumerate((y_right, y_left))]
    for copy in ring:
        copy.start()
    grecv[pl.ds(slice_me, 1)] = gsend[pl.ds(slice_me, 1)]

    grad_sup = (1.0 - BETA_MIX) * grad_pre + BETA_MIX * mm(grad_low, w[...], ((1,), (1,)))
    grad_agg = ((1.0 - ALPHA_MIX) * grad_sup).astype(BF)
    g = [grad_agg[0:TILE, :], grad_agg[TILE:, :]]
    for q in range(2):
        total = mm(tiles[q, 0], g[q], ((0,), (0,)))
        at, found = jnp.int32(0), jnp.int32(0)
        for k in range(1, K):
            same = cols[1 - q, k] == q
            at, found = jnp.where(same, k, at), jnp.where(same, 1, found)
        other = jnp.where(jnp.full((TILE, TILE), found, I32) > 0, tiles[1 - q, at].astype(F32), 0.0).astype(BF)
        total = total + mm(other, g[1 - q], ((0,), (0,)))
        rows = slice(q * TILE, (q + 1) * TILE)
        gx_o[rows, :] = jnp.where(live[rows, :] > 0, total, 0.0).astype(BF)

    wait_bytes(grecv.at[pl.ds(0, GROUP - 1)], rs_r)
    zsend[...] = jnp.sum(grecv[...].astype(F32), axis=0).astype(BF)
    for device in z_peers():
        remote(zsend, zrecv.at[z], z_s, z_r, device).start()
    zrecv[pl.ds(z, 1)] = zsend[...].reshape(1, H // GROUP, H)

    half = ROWS // 2
    ring[0].wait_recv()
    before, after = lax.rem(b + Y - 1, Y), lax.rem(b + 1, Y)
    on = [
        remote(outs.at[before, pl.ds(0, half)], outs.at[before, pl.ds(0, half)], y_s.at[2], y_r.at[2], y_right),
        remote(outs.at[after, pl.ds(half, half)], outs.at[after, pl.ds(half, half)], y_s.at[3], y_r.at[3], y_left),
    ]
    on[0].start()
    ring[1].wait_recv()
    on[1].start()
    for copy in on:
        copy.wait_recv()

    stores = []

    def scatter(i):
        rows = pl.ds(i * CHUNK, CHUNK)
        new = hist[rows, :].astype(F32) + mm(place[rows, :], outs[...].reshape(PART, H))
        hist[rows, :] = new.astype(BF)
        store = pltpu.make_async_copy(hist.at[rows], nh_o.at[rows], out_sem.at[i])
        store.start()
        stores.append(store)

    for i in range(4):
        scatter(i)
    wait_bytes(zrecv.at[pl.ds(0, Z - 1)], z_r)
    scale = BETA_MIX / (N_DOM * Y)
    asend[...] = (scale * jnp.sum(zrecv[...].astype(F32), axis=0)).astype(BF)
    for _, device in peers:
        remote(asend, arecv.at[slice_me], ag_s, ag_r, device).start()
    arecv[pl.ds(slice_me, 1)] = asend[...].reshape(1, H // GROUP, H)
    for i in range(4, HIST // CHUNK):
        scatter(i)

    for copy in near_req + near_row + ring + on:
        copy.wait_send()
    wait_bytes(wreq.at[pl.ds(0, N_DOM - 1)], req_s)
    wait_bytes(rbuf.at[pl.ds(0, N_DOM - 1)], row_s)
    wait_bytes(grecv.at[pl.ds(0, GROUP - 1)], rs_s)
    wait_bytes(zrecv.at[pl.ds(0, Z - 1)], z_s)
    wait_bytes(arecv.at[pl.ds(0, GROUP - 1)], ag_s)
    for store in stores:
        store.wait()
    wait_bytes(arecv.at[pl.ds(0, GROUP - 1)], ag_r)
    gw_o[...] = arecv[...].astype(F32).reshape(H, H)


def hand_on(nh_i, gx_i, gw_i, nh_o, gx_o, gw_o, nh, gx, gw, sem_in, sem_out):
    parts = [(nh_i.at[pl.ds(i * 1024, 1024)], nh.at[pl.ds(i * 1024, 1024)], nh_o.at[pl.ds(i * 1024, 1024)]) for i in range(4)]
    parts = [(gw_i, gw, gw_o), (gx_i, gx, gx_o), *parts]
    come = [pltpu.make_async_copy(src, mid, sem_in.at[i]) for i, (src, mid, _) in enumerate(parts)]
    go = [pltpu.make_async_copy(mid, dst, sem_out.at[i]) for i, (_, mid, dst) in enumerate(parts)]
    for copy in come:
        copy.start()
    for first, then in zip(come, go):
        first.wait()
        then.start()
    for copy in go:
        copy.wait()


def shards(features, initial, grad_output, weight, history, halo_table, tile_cols, tile_vals, batch_ids):
    hbm = pl.BlockSpec(memory_space=pl.ANY)
    vmem = pl.BlockSpec(memory_space=pltpu.VMEM)
    v = pltpu.VMEM
    dma = pltpu.SemaphoreType.DMA
    table = jnp.transpose(halo_table[0, 0])
    shapes = (
        jax.ShapeDtypeStruct((HIST, H), BF),
        jax.ShapeDtypeStruct((ROWS, H), BF),
        jax.ShapeDtypeStruct((H, H), F32),
    )
    piece = H // GROUP
    parts = pl.pallas_call(
        kernel,
        out_shape=shapes,
        in_specs=[hbm] * 9,
        out_specs=(hbm, vmem, vmem),
        scratch_shapes=[
            v((CAP, N_DOM), I32), v((Y, ROWS), I32), pltpu.SMEM((2, K), I32), v((HIST, H), BF), v((ROWS, H), BF),
            v((ROWS, H), BF), v((ROWS, H), BF), v((H, H), BF), v((2, K, TILE, TILE), BF),
            v((1, N_DOM), I32), v((N_DOM, 1, N_DOM), I32), v((2, CAP, N_DOM), I32),
            v((N_DOM, 4, TILE), BF), v((N_DOM, 4, TILE), BF), v((2, CAP, H), BF), v((2, CAP, H), BF),
            v((4 * N_DOM, 4 * N_DOM), BF), v((N_DOM * CAP, 4 * N_DOM), BF), v((N_DOM * CAP, 4 * N_DOM), BF),
            v((N_DOM * CAP, 32), BF), v((HIST, PART), BF), v((NB, TILE, H), BF), v((ROWS, H), F32),
            v((Y, ROWS, H), BF), v((GROUP, piece, H), BF), v((GROUP, piece, H), BF), v((piece, H), BF),
            v((Z, piece, H), BF), v((piece, H), BF), v((GROUP, piece, H), BF),
            dma((9,)), dma(()), dma(()), dma((2,)), dma((2,)), dma(()), dma(()), dma((2,)), dma((2,)),
            dma(()), dma(()), dma(()), dma(()), dma(()), dma(()), dma((4,)), dma((4,)), dma((HIST // CHUNK,)),
        ],
        compiler_params=pltpu.CompilerParams(collective_id=0, has_side_effects=True, vmem_limit_bytes=60 * 1024 * 1024),
        name="layer",
    )(table, batch_ids[0], tile_cols[0, 0], history[0], features[0], initial[0], grad_output[0], weight, tile_vals[0, 0])
    new_hist, grad_x, grad_w = pl.pallas_call(
        hand_on,
        out_shape=shapes,
        in_specs=[hbm] * 3,
        out_specs=(hbm, hbm, hbm),
        scratch_shapes=[v((HIST, H), BF), v((ROWS, H), BF), v((H, H), F32), dma((6,)), dma((6,))],
        compiler_params=pltpu.CompilerParams(vmem_limit_bytes=60 * 1024 * 1024),
        name="hand_on",
    )(*parts)
    return new_hist[None], grad_x[None], grad_w


def solution(mesh):
    return jax.shard_map(
        shards,
        mesh=mesh,
        in_specs=(
            P("dom", "batch", None),
            P("dom", "batch", None),
            P("dom", "batch", None),
            P(),
            P("dom", None, None),
            P("dom", "batch", None, None),
            P("dom", "batch", None, None),
            P("dom", "batch", None, None, None, None),
            P("dom", None, None),
        ),
        out_specs=(P("dom", None, None), P("dom", "batch", None), P()),
        check_vma=False,
    )
```

```python
import math

import jax
import jax.numpy as jnp
from jax import lax
from jax.experimental import pallas as pl
from jax.experimental.pallas import tpu as pltpu
from jax.sharding import PartitionSpec as P

ALPHA_MIX = 0.1
BETA_MIX = math.log(1.5)
X, Z, C, Y = 4, 16, 2, 4
N_DOM = X * Z * C
GROUP = X * Y * C
H = 256
TILE = 128
ROWS = 256
HIST = 4096
CAP = 8
K = 8
NB = 2 + N_DOM * CAP // TILE
PART = Y * ROWS
BASE = 8192
CHUNK = 512
BF = jnp.bfloat16
F32 = jnp.float32
I32 = jnp.int32


def coords():
    d = lax.axis_index("dom")
    return lax.div(d, Z * C), lax.rem(lax.div(d, C), Z), lax.rem(d, C), lax.axis_index("batch")


def dom_of(x, z, c):
    return (x * Z + z) * C + c


def each_dom_peer(fn):
    x, z, c, _ = coords()

    def plane(zz, own):
        for dx in (2, 1, 3, 0):
            for dc in (1, 0):
                if not (own and dx == 0 and dc == 0):
                    fn(dom_of(lax.rem(x + dx, X), zz, lax.rem(c + dc, C)))

    def body(k, carry):
        odd, half = lax.rem(k, 2), lax.div(k, 2)
        plane(lax.rem(z + Z // 2 + half * (1 - 2 * odd) - odd, Z), False)
        return carry

    lax.fori_loop(0, Z - 1, body, 0)
    plane(z, True)


def group_peers(skip_same_batch):
    x, z, c, b = coords()
    out = []
    for dx in (2, 1, 3, 0):
        for dy in (2, 1, 3, 0):
            for dc in (1, 0):
                if (dx, dy, dc) == (0, 0, 0) or (skip_same_batch and dy == 0):
                    continue
                qx, qy, qc = lax.rem(x + dx, X), lax.rem(b + dy, Y), lax.rem(c + dc, C)
                out.append(((qx * Y + qy) * C + qc, {"dom": dom_of(qx, z, qc), "batch": qy}))
    return out


def z_peers():
    x, z, c, _ = coords()
    return [{"dom": dom_of(x, lax.rem(z + i, Z), c)} for i in (8, 7, 9, 6, 10, 5, 11, 4, 12, 3, 13, 2, 14, 1, 15)]


def remote(src, dst, send, recv, device):
    return pltpu.make_async_remote_copy(src_ref=src, dst_ref=dst, send_sem=send, recv_sem=recv, device_id=device)


def wait_bytes(like, sem):
    pltpu.make_async_copy(like, like, sem).wait()


def iota(shape, dim):
    return lax.broadcasted_iota(I32, shape, dim)


def ones_where(mask):
    return jnp.where(mask, 1.0, 0.0).astype(BF)


def mm(a, b, dims=((1,), (0,))):
    return lax.dot_general(a, b, (dims, ((), ())), preferred_element_type=F32)


def kernel(
    tab_h, ids_h, cols_h, hist_h, feat_h, init_h, gout_h, w_h, tiles_h,
    nh_o, gx_o, gw_o,
    tab, ids, cols, hist, feat, init, gout, w, tiles,
    req, wreq, ntab, mixed, sbuf, rbuf, nsend, nrow, adj, adj_far, adj_near, place, base, live,
    outs, gsend, grecv, zsend, zrecv, asend, arecv,
    in_sem, req_s, req_r, nreq_s, nreq_r, row_s, row_r, nrow_s, nrow_r, rs_s, rs_r, z_s, z_r, ag_s, ag_r, y_s, y_r,
):
    x, z, c, b = coords()
    me = lax.axis_index("dom")
    pairs = [
        (tab_h, tab), (ids_h, ids), (cols_h, cols), (hist_h, hist), (feat_h, feat),
        (init_h, init), (gout_h, gout), (w_h, w), (tiles_h, tiles),
    ]
    loads = [pltpu.make_async_copy(src, dst, in_sem.at[i]) for i, (src, dst) in enumerate(pairs)]
    loads[0].start()
    barrier = pltpu.get_barrier_semaphore()
    each_dom_peer(lambda p: pl.semaphore_signal(barrier, inc=1, device_id={"dom": p}))
    others = group_peers(True)
    for _, device in others:
        pl.semaphore_signal(barrier, inc=1, device_id=device)
    for load in loads[1:]:
        load.start()

    loads[0].wait()
    req[...] = (tab[0:1, :] + 1) * BASE + (tab[1:2, :] + 1)
    wreq[pl.ds(me, 1)] = jnp.zeros((1, 1, N_DOM), I32)
    right, left = lax.rem(me + 1, N_DOM), lax.rem(me + N_DOM - 1, N_DOM)
    pl.semaphore_wait(barrier, N_DOM - 1 + len(others))
    near_req = [remote(tab, ntab.at[i], nreq_s.at[i], nreq_r.at[i], {"dom": p}) for i, p in enumerate((right, left))]
    for copy in near_req:
        copy.start()
    each_dom_peer(lambda p: remote(req, wreq.at[me], req_s, req_r, {"dom": p}).start())

    loads[1].wait()

    def place_chunk(i, carry):
        rows = iota((CHUNK, ROWS), 0) + i * CHUNK
        for q in range(Y):
            place[pl.ds(pl.multiple_of(i * CHUNK, CHUNK), CHUNK), pl.ds(q * ROWS, ROWS)] = ones_where(rows == ids[q : q + 1, :])
        return carry

    lax.fori_loop(0, HIST // CHUNK, place_chunk, 0)
    loads[3].wait()

    wait_bytes(wreq.at[pl.ds(0, N_DOM - 1)], req_r)
    for copy in near_req:
        copy.wait_recv()

    lane_me = iota((1, N_DOM), 1) == me

    def column(v):
        return jnp.sum(jnp.where(lane_me, v.astype(F32), 0.0), axis=1, keepdims=True)

    asked = wreq[...].reshape(N_DOM, N_DOM)
    wanted = jnp.concatenate(
        [
            column(lax.shift_right_logical(asked, 13) - 1),
            column(jnp.bitwise_and(asked, BASE - 1) - 1),
            column(tab[...]),
            column(ntab[0]),
            column(ntab[1]),
            jnp.full((8, 1), -1.0, F32),
        ],
        axis=0,
    ).astype(I32)
    n_ask = 2 * N_DOM + 32
    got = jnp.zeros((n_ask, H), F32)
    for i in range(HIST // CHUNK):
        hot = ones_where(wanted == iota((n_ask, CHUNK), 1) + i * CHUNK)
        got = got + mm(hot, hist[pl.ds(i * CHUNK, CHUNK), :])
    n0 = 2 * N_DOM
    nsend[0] = got[n0 + 16 : n0 + 24, :].astype(BF)
    nsend[1] = got[n0 + 8 : n0 + 16, :].astype(BF)
    near_row = [remote(nsend.at[i], nrow.at[i], nrow_s.at[i], nrow_r.at[i], {"dom": p}) for i, p in enumerate((right, left))]
    for copy in near_row:
        copy.start()
    for i in range(2):
        for j in range(2):
            mixed[j, pl.ds(i, N_DOM, 2), :] = got[i * N_DOM : (i + 1) * N_DOM, j * TILE : (j + 1) * TILE]
    sbuf[...] = jnp.concatenate([mixed[0], mixed[1]], axis=1).astype(BF).reshape(N_DOM, 2, H)
    rbuf[pl.ds(me, 1)] = jnp.zeros((1, 2, H), BF)
    each_dom_peer(lambda p: remote(sbuf.at[p], rbuf.at[me], row_s, row_r, {"dom": p}).start())

    own_rows = got[n0 : n0 + 8, :]
    for i in (2, 8):
        loads[i].wait()
    for r in range(2):
        for col in range(NB):
            at, found = jnp.int32(0), jnp.int32(1 if col == r else 0)
            for k in range(1, K if col != r else 1):
                same = cols[r, k] == col
                at, found = jnp.where(same, k, at), jnp.where(same, 1, found)
            tile = tiles[r, at]
            if col != r:
                tile = jnp.where(jnp.full((TILE, TILE), found, I32) > 0, tile.astype(F32), 0.0).astype(BF)
            adj[r * TILE : (r + 1) * TILE, col * TILE : (col + 1) * TILE] = tile
    shape = (N_DOM * CAP, 2 * N_DOM)
    p_row, p_col = iota(shape, 0), iota(shape, 1)
    slot = lax.rem(p_row, CAP)
    spread = ones_where(p_col == jnp.where(slot < 2, p_row // CAP * 2 + slot, -1))
    adj_far[...] = mm(adj[:, 2 * TILE :], spread).astype(BF)
    shape = (N_DOM * CAP, 32)
    p_row, p_col = iota(shape, 0), iota(shape, 1)
    who, slot = p_col // 8, lax.rem(p_col, 8)
    owner = jnp.where(who == 0, me, jnp.where(who == 1, left, right))
    spread = ones_where((p_row == owner * CAP + slot) & (who < 3) & ((who == 0) | (slot >= 2)))
    adj_near[...] = mm(adj[:, 2 * TILE :], spread).astype(BF)
    mine = jnp.sum(jnp.where(iota((Y, ROWS), 0) == b, (ids[...] >= 0).astype(F32), 0.0), axis=0, keepdims=True)
    live_col = jnp.sum(jnp.where(iota((ROWS, ROWS), 0) == iota((ROWS, ROWS), 1), mine, 0.0), axis=1, keepdims=True)
    live[...] = jnp.broadcast_to(live_col, (ROWS, H))
    loads[4].wait()
    loads[5].wait()
    masked = jnp.where(live[...] > 0, feat[...].astype(F32), 0.0).astype(BF)
    base[...] = (1.0 - ALPHA_MIX) * mm(adj[:, 0 : 2 * TILE], masked) + ALPHA_MIX * init[...].astype(F32)

    def clear_chunk(i, carry):
        rows = pl.ds(pl.multiple_of(i * CHUNK, CHUNK), CHUNK)
        hit = jnp.max(place[rows, :].astype(F32), axis=1, keepdims=True)
        nh_o[rows, :] = jnp.where(hit > 0, 0.0, hist[rows, :].astype(F32)).astype(BF)
        return carry

    lax.fori_loop(0, HIST // CHUNK, clear_chunk, 0)
    for i in (6, 7):
        loads[i].wait()

    for copy in near_row:
        copy.wait_recv()
    wait_bytes(rbuf.at[pl.ds(0, N_DOM - 1)], row_r)

    near = jnp.concatenate([own_rows, nrow[0].astype(F32), nrow[1].astype(F32), jnp.zeros((8, H), F32)], axis=0).astype(BF)

    halo = mm(adj_far[...], rbuf[...].reshape(2 * N_DOM, H)) + mm(adj_near[...], near)
    support = base[...] + (1.0 - ALPHA_MIX) * halo
    support_low = support.astype(BF)
    pre_act = (1.0 - BETA_MIX) * support + BETA_MIX * mm(support_low, w[...])
    sig = jax.nn.sigmoid(pre_act)
    slope = gout[...].astype(F32) * sig * (1.0 + pre_act * (1.0 - sig))
    grad_pre = jnp.where(live[...] > 0, slope, 0.0)
    grad_low = grad_pre.astype(BF)
    grad_w = mm(support_low, grad_low, ((0,), (0,)))

    gsend[...] = grad_w.astype(BF).reshape(GROUP, H // GROUP, H)
    slice_me = (x * Y + b) * C + c
    peers = group_peers(False)
    for slot_q, device in peers:
        remote(gsend.at[slot_q], grecv.at[slice_me], rs_s, rs_r, device).start()
    outs[pl.ds(b, 1)] = (pre_act * sig).astype(BF).reshape(1, ROWS, H)
    grecv[pl.ds(slice_me, 1)] = gsend[pl.ds(slice_me, 1)]

    grad_sup = (1.0 - BETA_MIX) * grad_pre + BETA_MIX * mm(grad_low, w[...], ((1,), (1,)))
    grad_agg = ((1.0 - ALPHA_MIX) * grad_sup).astype(BF)
    grad_x = mm(adj[:, 0 : 2 * TILE], grad_agg, ((0,), (0,)))
    gx_o[...] = jnp.where(live[...] > 0, grad_x, 0.0).astype(BF)

    wait_bytes(grecv.at[pl.ds(0, GROUP - 1)], rs_r)
    zsend[...] = jnp.sum(grecv[...].astype(F32), axis=0).astype(BF)
    for device in z_peers():
        remote(zsend, zrecv.at[z], z_s, z_r, device).start()
    zrecv[pl.ds(z, 1)] = zsend[...].reshape(1, H // GROUP, H)

    y_right, y_left = {"batch": lax.rem(b + 1, Y)}, {"batch": lax.rem(b + Y - 1, Y)}
    ring = [remote(outs.at[b], outs.at[b], y_s.at[i], y_r.at[i], p) for i, p in enumerate((y_right, y_left))]
    for copy in ring:
        copy.start()

    def scatter(q):
        lanes = pl.ds(pl.multiple_of(q * ROWS, ROWS), ROWS)
        for i in range(HIST // CHUNK):
            rows = pl.ds(i * CHUNK, CHUNK)
            nh_o[rows, :] = (nh_o[rows, :].astype(F32) + mm(place[rows, lanes], outs[q])).astype(BF)

    scatter(b)
    half = ROWS // 2
    before, after = lax.rem(b + Y - 1, Y), lax.rem(b + 1, Y)
    on = [
        remote(outs.at[before, pl.ds(0, half)], outs.at[before, pl.ds(0, half)], y_s.at[2], y_r.at[2], y_right),
        remote(outs.at[after, pl.ds(half, half)], outs.at[after, pl.ds(half, half)], y_s.at[3], y_r.at[3], y_left),
    ]
    ring[0].wait_recv()
    on[0].start()
    ring[1].wait_recv()
    on[1].start()
    scatter(before)
    wait_bytes(zrecv.at[pl.ds(0, Z - 1)], z_r)
    scale = BETA_MIX / (N_DOM * Y)
    asend[...] = (scale * jnp.sum(zrecv[...].astype(F32), axis=0)).astype(BF)
    for _, device in peers:
        remote(asend, arecv.at[slice_me], ag_s, ag_r, device).start()
    arecv[pl.ds(slice_me, 1)] = asend[...].reshape(1, H // GROUP, H)
    scatter(after)
    for copy in on:
        copy.wait_recv()
    scatter(lax.rem(b + 2, Y))

    for copy in near_req + near_row + ring + on:
        copy.wait_send()
    wait_bytes(wreq.at[pl.ds(0, N_DOM - 1)], req_s)
    wait_bytes(rbuf.at[pl.ds(0, N_DOM - 1)], row_s)
    wait_bytes(grecv.at[pl.ds(0, GROUP - 1)], rs_s)
    wait_bytes(zrecv.at[pl.ds(0, Z - 1)], z_s)
    wait_bytes(arecv.at[pl.ds(0, GROUP - 1)], ag_s)
    wait_bytes(arecv.at[pl.ds(0, GROUP - 1)], ag_r)
    gw_o[...] = arecv[...].astype(F32).reshape(H, H)


def hand_on(nh_i, gx_i, gw_i, nh_o, gx_o, gw_o, sem):
    step = HIST // 4
    parts = [(gw_i, gw_o), (gx_i, gx_o)]
    parts += [(nh_i.at[pl.ds(i * step, step)], nh_o.at[pl.ds(i * step, step)]) for i in range(4)]
    copies = [pltpu.make_async_copy(src, dst, sem.at[i]) for i, (src, dst) in enumerate(parts)]
    for copy in copies:
        copy.start()
    for copy in copies:
        copy.wait()


def shards(features, initial, grad_output, weight, history, halo_table, tile_cols, tile_vals, batch_ids):
    hbm = pl.BlockSpec(memory_space=pl.ANY)
    vmem = pl.BlockSpec(memory_space=pltpu.VMEM)
    v = pltpu.VMEM
    dma = pltpu.SemaphoreType.DMA
    table = jnp.transpose(halo_table[0, 0])
    shapes = (
        jax.ShapeDtypeStruct((HIST, H), BF),
        jax.ShapeDtypeStruct((ROWS, H), BF),
        jax.ShapeDtypeStruct((H, H), F32),
    )
    piece = H // GROUP
    parts = pl.pallas_call(
        kernel,
        out_shape=(v((HIST, H), BF), v((ROWS, H), BF), v((H, H), F32)),
        in_specs=[hbm] * 9,
        out_specs=(vmem, vmem, vmem),
        scratch_shapes=[
            v((CAP, N_DOM), I32), v((Y, ROWS), I32), pltpu.SMEM((2, K), I32), v((HIST, H), BF), v((ROWS, H), BF),
            v((ROWS, H), BF), v((ROWS, H), BF), v((H, H), BF), v((2, K, TILE, TILE), BF),
            v((1, N_DOM), I32), v((N_DOM, 1, N_DOM), I32), v((2, CAP, N_DOM), I32),
            v((2, 2 * N_DOM, TILE), F32), v((N_DOM, 2, H), BF), v((N_DOM, 2, H), BF), v((2, CAP, H), BF), v((2, CAP, H), BF),
            v((ROWS, NB * TILE), BF), v((ROWS, 2 * N_DOM), BF), v((ROWS, 32), BF), v((HIST, PART), BF),
            v((ROWS, H), F32), v((ROWS, H), F32),
            v((Y, ROWS, H), BF), v((GROUP, piece, H), BF), v((GROUP, piece, H), BF), v((piece, H), BF),
            v((Z, piece, H), BF), v((piece, H), BF), v((GROUP, piece, H), BF),
            dma((9,)), dma(()), dma(()), dma((2,)), dma((2,)), dma(()), dma(()), dma((2,)), dma((2,)),
            dma(()), dma(()), dma(()), dma(()), dma(()), dma(()), dma((4,)), dma((4,)),
        ],
        compiler_params=pltpu.CompilerParams(collective_id=0, has_side_effects=True, vmem_limit_bytes=40 * 1024 * 1024),
        name="layer",
    )(*[
        pltpu.with_memory_space_constraint(a, pltpu.HBM)
        for a in (
            table, batch_ids[0], tile_cols[0, 0], history[0], features[0], initial[0], grad_output[0], weight, tile_vals[0, 0],
        )
    ])
    new_hist, grad_x, grad_w = pl.pallas_call(
        hand_on,
        out_shape=shapes,
        in_specs=[vmem] * 3,
        out_specs=(hbm, hbm, hbm),
        scratch_shapes=[dma((6,))],
        compiler_params=pltpu.CompilerParams(vmem_limit_bytes=16 * 1024 * 1024),
        name="hand_on",
    )(*[pltpu.with_memory_space_constraint(a, pltpu.VMEM) for a in parts])
    return new_hist[None], grad_x[None], grad_w


def solution(mesh):
    return jax.shard_map(
        shards,
        mesh=mesh,
        in_specs=(
            P("dom", "batch", None),
            P("dom", "batch", None),
            P("dom", "batch", None),
            P(),
            P("dom", None, None),
            P("dom", "batch", None, None),
            P("dom", "batch", None, None),
            P("dom", "batch", None, None, None, None),
            P("dom", None, None),
        ),
        out_specs=(P("dom", None, None), P("dom", "batch", None), P()),
        check_vma=False,
    )
```

```python
import math

import jax
import jax.numpy as jnp
from jax import lax
from jax.experimental import pallas as pl
from jax.experimental.pallas import tpu as pltpu
from jax.sharding import PartitionSpec as P

ALPHA_MIX = 0.1
BETA_MIX = math.log(1.5)
X, Z, C, Y = 4, 16, 2, 4
N_DOM = X * Z * C
GROUP = X * Y * C
H = 256
TILE = 128
ROWS = 256
HIST = 4096
CAP = 8
K = 8
NB = 2 + N_DOM * CAP // TILE
PART = Y * ROWS
BASE = 8192
CHUNK = 512
BF = jnp.bfloat16
F32 = jnp.float32
I32 = jnp.int32


def coords():
    d = lax.axis_index("dom")
    return lax.div(d, Z * C), lax.rem(lax.div(d, C), Z), lax.rem(d, C), lax.axis_index("batch")


def dom_of(x, z, c):
    return (x * Z + z) * C + c


def each_dom_peer(fn):
    x, z, c, _ = coords()

    def plane(zz, own):
        for dx in (2, 1, 3, 0):
            for dc in (1, 0):
                if not (own and dx == 0 and dc == 0):
                    fn(dom_of(lax.rem(x + dx, X), zz, lax.rem(c + dc, C)))

    def body(k, carry):
        odd, half = lax.rem(k, 2), lax.div(k, 2)
        plane(lax.rem(z + Z // 2 + half * (1 - 2 * odd) - odd, Z), False)
        return carry

    lax.fori_loop(0, Z - 1, body, 0)
    plane(z, True)


def group_peers(skip_same_batch):
    x, z, c, b = coords()
    out = []
    for dx in (2, 1, 3, 0):
        for dy in (2, 1, 3, 0):
            for dc in (1, 0):
                if (dx, dy, dc) == (0, 0, 0) or (skip_same_batch and dy == 0):
                    continue
                qx, qy, qc = lax.rem(x + dx, X), lax.rem(b + dy, Y), lax.rem(c + dc, C)
                out.append(((qx * Y + qy) * C + qc, {"dom": dom_of(qx, z, qc), "batch": qy}))
    return out


def z_peers():
    x, z, c, _ = coords()
    return [{"dom": dom_of(x, lax.rem(z + i, Z), c)} for i in (8, 7, 9, 6, 10, 5, 11, 4, 12, 3, 13, 2, 14, 1, 15)]


def remote(src, dst, send, recv, device):
    return pltpu.make_async_remote_copy(src_ref=src, dst_ref=dst, send_sem=send, recv_sem=recv, device_id=device)


def wait_bytes(like, sem):
    pltpu.make_async_copy(like, like, sem).wait()


def iota(shape, dim):
    return lax.broadcasted_iota(I32, shape, dim)


def ones_where(mask):
    return jnp.where(mask, 1.0, 0.0).astype(BF)


def mm(a, b, dims=((1,), (0,))):
    return lax.dot_general(a, b, (dims, ((), ())), preferred_element_type=F32)


def kernel(
    tab_h, ids_h, cols_h, hist_h, feat_h, init_h, gout_h, w_h, tiles_h,
    nh_o, gx_o, gw_o,
    tab, ids, cols, hist, feat, init, gout, w, tiles,
    req, wreq, ntab, mixed, sbuf, rbuf, nsend, nrow, adj, adj_far, adj_near, place, base, live,
    outs, gsend, grecv, zsend, zrecv, asend, arecv,
    in_sem, req_s, req_r, nreq_s, nreq_r, row_s, row_r, nrow_s, nrow_r, rs_s, rs_r, z_s, z_r, ag_s, ag_r, y_s, y_r,
):
    x, z, c, b = coords()
    me = lax.axis_index("dom")
    pairs = [
        (tab_h, tab), (ids_h, ids), (cols_h, cols), (hist_h, hist), (feat_h, feat),
        (init_h, init), (gout_h, gout), (w_h, w), (tiles_h, tiles),
    ]
    loads = [pltpu.make_async_copy(src, dst, in_sem.at[i]) for i, (src, dst) in enumerate(pairs)]
    loads[0].start()
    barrier = pltpu.get_barrier_semaphore()
    each_dom_peer(lambda p: pl.semaphore_signal(barrier, inc=1, device_id={"dom": p}))
    others = group_peers(True)
    for _, device in others:
        pl.semaphore_signal(barrier, inc=1, device_id=device)
    for load in loads[1:]:
        load.start()

    loads[0].wait()
    req[...] = (tab[0:1, :] + 1) * BASE + (tab[1:2, :] + 1)
    wreq[pl.ds(me, 1)] = jnp.zeros((1, 1, N_DOM), I32)
    right, left = lax.rem(me + 1, N_DOM), lax.rem(me + N_DOM - 1, N_DOM)
    pl.semaphore_wait(barrier, N_DOM - 1 + len(others))
    near_req = [remote(tab, ntab.at[i], nreq_s.at[i], nreq_r.at[i], {"dom": p}) for i, p in enumerate((right, left))]
    each_dom_peer(lambda p: remote(req, wreq.at[me], req_s, req_r, {"dom": p}).start())
    for copy in near_req:
        copy.start()

    loads[1].wait()

    def place_chunk(i, carry):
        rows = iota((CHUNK, ROWS), 0) + i * CHUNK
        for q in range(Y):
            place[pl.ds(pl.multiple_of(i * CHUNK, CHUNK), CHUNK), pl.ds(q * ROWS, ROWS)] = ones_where(rows == ids[q : q + 1, :])
        return carry

    lax.fori_loop(0, HIST // CHUNK, place_chunk, 0)
    loads[3].wait()

    wait_bytes(wreq.at[pl.ds(0, N_DOM - 1)], req_r)
    for copy in near_req:
        copy.wait_recv()

    lane_me = iota((1, N_DOM), 1) == me

    def column(v):
        return jnp.sum(jnp.where(lane_me, v.astype(F32), 0.0), axis=1, keepdims=True)

    asked = wreq[...].reshape(N_DOM, N_DOM)
    wanted = jnp.concatenate(
        [
            column(lax.shift_right_logical(asked, 13) - 1),
            column(jnp.bitwise_and(asked, BASE - 1) - 1),
            column(tab[...]),
            column(ntab[0]),
            column(ntab[1]),
            jnp.full((8, 1), -1.0, F32),
        ],
        axis=0,
    ).astype(I32)
    n_ask = 2 * N_DOM + 32
    block = jnp.where((wanted & 255) == iota((n_ask, 256), 1), (wanted >> 8).astype(F32), -1.0).astype(BF)
    def part(first, last):
        hot = jnp.concatenate([jnp.where(block[first:last] == BF(i), BF(1), BF(0)) for i in range(HIST // 256)], axis=1)
        return mm(hot, hist[...])

    got = jnp.concatenate([part(0, 144), part(144, 288)], axis=0)
    n0 = 2 * N_DOM
    nsend[0] = got[n0 + 16 : n0 + 24, :].astype(BF)
    nsend[1] = got[n0 + 8 : n0 + 16, :].astype(BF)
    near_row = [remote(nsend.at[i], nrow.at[i], nrow_s.at[i], nrow_r.at[i], {"dom": p}) for i, p in enumerate((right, left))]
    for i in range(2):
        for j in range(2):
            mixed[j, pl.ds(i, N_DOM, 2), :] = got[i * N_DOM : (i + 1) * N_DOM, j * TILE : (j + 1) * TILE]
    sbuf[...] = jnp.concatenate([mixed[0], mixed[1]], axis=1).astype(BF).reshape(N_DOM, 2, H)
    rbuf[pl.ds(me, 1)] = jnp.zeros((1, 2, H), BF)
    each_dom_peer(lambda p: remote(sbuf.at[p], rbuf.at[me], row_s, row_r, {"dom": p}).start())
    for copy in near_row:
        copy.start()

    own_rows = got[n0 : n0 + 8, :]
    for i in (2, 8):
        loads[i].wait()
    for r in range(2):
        for col in range(NB):
            at, found = jnp.int32(0), jnp.int32(1 if col == r else 0)
            for k in range(1, K if col != r else 1):
                same = cols[r, k] == col
                at, found = jnp.where(same, k, at), jnp.where(same, 1, found)
            tile = tiles[r, at]
            if col != r:
                tile = jnp.where(jnp.full((TILE, TILE), found, I32) > 0, tile.astype(F32), 0.0).astype(BF)
            adj[r * TILE : (r + 1) * TILE, col * TILE : (col + 1) * TILE] = tile
    shape = (N_DOM * CAP, 2 * N_DOM)
    p_row, p_col = iota(shape, 0), iota(shape, 1)
    slot = lax.rem(p_row, CAP)
    spread = ones_where(p_col == jnp.where(slot < 2, p_row // CAP * 2 + slot, -1))
    adj_far[...] = mm(adj[:, 2 * TILE :], spread).astype(BF)
    shape = (N_DOM * CAP, 32)
    p_row, p_col = iota(shape, 0), iota(shape, 1)
    who, slot = p_col // 8, lax.rem(p_col, 8)
    owner = jnp.where(who == 0, me, jnp.where(who == 1, left, right))
    spread = ones_where((p_row == owner * CAP + slot) & (who < 3) & ((who == 0) | (slot >= 2)))
    adj_near[...] = mm(adj[:, 2 * TILE :], spread).astype(BF)
    mine = jnp.sum(jnp.where(iota((Y, ROWS), 0) == b, (ids[...] >= 0).astype(F32), 0.0), axis=0, keepdims=True)
    live_col = jnp.sum(jnp.where(iota((ROWS, ROWS), 0) == iota((ROWS, ROWS), 1), mine, 0.0), axis=1, keepdims=True)
    live[...] = jnp.broadcast_to(live_col, (ROWS, H))
    loads[4].wait()
    loads[5].wait()
    masked = jnp.where(live[...] > 0, feat[...].astype(F32), 0.0).astype(BF)
    base[...] = (1.0 - ALPHA_MIX) * mm(adj[:, 0 : 2 * TILE], masked) + ALPHA_MIX * init[...].astype(F32)

    def clear_chunk(i, carry):
        rows = pl.ds(pl.multiple_of(i * CHUNK, CHUNK), CHUNK)
        hit = jnp.max(place[rows, :].astype(F32), axis=1, keepdims=True)
        nh_o[rows, :] = jnp.where(hit > 0, 0.0, hist[rows, :].astype(F32)).astype(BF)
        return carry

    lax.fori_loop(0, HIST // CHUNK, clear_chunk, 0)
    for i in (6, 7):
        loads[i].wait()

    for copy in near_row:
        copy.wait_recv()
    wait_bytes(rbuf.at[pl.ds(0, N_DOM - 1)], row_r)

    near = jnp.concatenate([own_rows, nrow[0].astype(F32), nrow[1].astype(F32), jnp.zeros((8, H), F32)], axis=0).astype(BF)

    halo = mm(adj_far[...], rbuf[...].reshape(2 * N_DOM, H)) + mm(adj_near[...], near)
    support = base[...] + (1.0 - ALPHA_MIX) * halo
    support_low = support.astype(BF)
    pre_act = (1.0 - BETA_MIX) * support + BETA_MIX * mm(support_low, w[...])
    sig = jax.nn.sigmoid(pre_act)
    slope = gout[...].astype(F32) * sig * (1.0 + pre_act * (1.0 - sig))
    grad_pre = jnp.where(live[...] > 0, slope, 0.0)
    grad_low = grad_pre.astype(BF)
    grad_w = mm(support_low, grad_low, ((0,), (0,)))

    gsend[...] = grad_w.astype(BF).reshape(GROUP, H // GROUP, H)
    slice_me = (x * Y + b) * C + c
    peers = group_peers(False)
    for slot_q, device in peers:
        remote(gsend.at[slot_q], grecv.at[slice_me], rs_s, rs_r, device).start()
    outs[pl.ds(b, 1)] = (pre_act * sig).astype(BF).reshape(1, ROWS, H)
    grecv[pl.ds(slice_me, 1)] = gsend[pl.ds(slice_me, 1)]

    grad_sup = (1.0 - BETA_MIX) * grad_pre + BETA_MIX * mm(grad_low, w[...], ((1,), (1,)))
    grad_agg = ((1.0 - ALPHA_MIX) * grad_sup).astype(BF)
    grad_x = mm(adj[:, 0 : 2 * TILE], grad_agg, ((0,), (0,)))
    gx_o[...] = jnp.where(live[...] > 0, grad_x, 0.0).astype(BF)

    wait_bytes(grecv.at[pl.ds(0, GROUP - 1)], rs_r)
    zsend[...] = jnp.sum(grecv[...].astype(F32), axis=0).astype(BF)
    for device in z_peers():
        remote(zsend, zrecv.at[z], z_s, z_r, device).start()
    zrecv[pl.ds(z, 1)] = zsend[...].reshape(1, H // GROUP, H)

    y_right, y_left = {"batch": lax.rem(b + 1, Y)}, {"batch": lax.rem(b + Y - 1, Y)}
    ring = [remote(outs.at[b], outs.at[b], y_s.at[i], y_r.at[i], p) for i, p in enumerate((y_right, y_left))]
    for copy in ring:
        copy.start()

    def scatter(q):
        lanes = pl.ds(pl.multiple_of(q * ROWS, ROWS), ROWS)
        for i in range(HIST // CHUNK):
            rows = pl.ds(i * CHUNK, CHUNK)
            nh_o[rows, :] = (nh_o[rows, :].astype(F32) + mm(place[rows, lanes], outs[q])).astype(BF)

    scatter(b)
    half = ROWS // 2
    before, after = lax.rem(b + Y - 1, Y), lax.rem(b + 1, Y)
    on = [
        remote(outs.at[before, pl.ds(0, half)], outs.at[before, pl.ds(0, half)], y_s.at[2], y_r.at[2], y_right),
        remote(outs.at[after, pl.ds(half, half)], outs.at[after, pl.ds(half, half)], y_s.at[3], y_r.at[3], y_left),
    ]
    ring[0].wait_recv()
    on[0].start()
    ring[1].wait_recv()
    on[1].start()
    scatter(before)
    wait_bytes(zrecv.at[pl.ds(0, Z - 1)], z_r)
    scale = BETA_MIX / (N_DOM * Y)
    asend[...] = (scale * jnp.sum(zrecv[...].astype(F32), axis=0)).astype(BF)
    for _, device in peers:
        remote(asend, arecv.at[slice_me], ag_s, ag_r, device).start()
    arecv[pl.ds(slice_me, 1)] = asend[...].reshape(1, H // GROUP, H)
    scatter(after)
    for copy in on:
        copy.wait_recv()
    scatter(lax.rem(b + 2, Y))

    for copy in near_req + near_row + ring + on:
        copy.wait_send()
    wait_bytes(wreq.at[pl.ds(0, N_DOM - 1)], req_s)
    wait_bytes(rbuf.at[pl.ds(0, N_DOM - 1)], row_s)
    wait_bytes(grecv.at[pl.ds(0, GROUP - 1)], rs_s)
    wait_bytes(zrecv.at[pl.ds(0, Z - 1)], z_s)
    wait_bytes(arecv.at[pl.ds(0, GROUP - 1)], ag_s)
    wait_bytes(arecv.at[pl.ds(0, GROUP - 1)], ag_r)
    gw_o[...] = arecv[...].astype(F32).reshape(H, H)


def hand_on(nh_i, gx_i, gw_i, nh_o, gx_o, gw_o, sem):
    step = HIST // 4
    parts = [(gw_i, gw_o), (gx_i, gx_o)]
    parts += [(nh_i.at[pl.ds(i * step, step)], nh_o.at[pl.ds(i * step, step)]) for i in range(4)]
    copies = [pltpu.make_async_copy(src, dst, sem.at[i]) for i, (src, dst) in enumerate(parts)]
    for copy in copies:
        copy.start()
    for copy in copies:
        copy.wait()


def shards(features, initial, grad_output, weight, history, halo_table, tile_cols, tile_vals, batch_ids):
    hbm = pl.BlockSpec(memory_space=pl.ANY)
    vmem = pl.BlockSpec(memory_space=pltpu.VMEM)
    v = pltpu.VMEM
    dma = pltpu.SemaphoreType.DMA
    table = jnp.transpose(halo_table[0, 0])
    shapes = (
        jax.ShapeDtypeStruct((HIST, H), BF),
        jax.ShapeDtypeStruct((ROWS, H), BF),
        jax.ShapeDtypeStruct((H, H), F32),
    )
    piece = H // GROUP
    parts = pl.pallas_call(
        kernel,
        out_shape=(v((HIST, H), BF), v((ROWS, H), BF), v((H, H), F32)),
        in_specs=[hbm] * 9,
        out_specs=(vmem, vmem, vmem),
        scratch_shapes=[
            v((CAP, N_DOM), I32), v((Y, ROWS), I32), pltpu.SMEM((2, K), I32), v((HIST, H), BF), v((ROWS, H), BF),
            v((ROWS, H), BF), v((ROWS, H), BF), v((H, H), BF), v((2, K, TILE, TILE), BF),
            v((1, N_DOM), I32), v((N_DOM, 1, N_DOM), I32), v((2, CAP, N_DOM), I32),
            v((2, 2 * N_DOM, TILE), F32), v((N_DOM, 2, H), BF), v((N_DOM, 2, H), BF), v((2, CAP, H), BF), v((2, CAP, H), BF),
            v((ROWS, NB * TILE), BF), v((ROWS, 2 * N_DOM), BF), v((ROWS, 32), BF), v((HIST, PART), BF),
            v((ROWS, H), F32), v((ROWS, H), F32),
            v((Y, ROWS, H), BF), v((GROUP, piece, H), BF), v((GROUP, piece, H), BF), v((piece, H), BF),
            v((Z, piece, H), BF), v((piece, H), BF), v((GROUP, piece, H), BF),
            dma((9,)), dma(()), dma(()), dma((2,)), dma((2,)), dma(()), dma(()), dma((2,)), dma((2,)),
            dma(()), dma(()), dma(()), dma(()), dma(()), dma(()), dma((4,)), dma((4,)),
        ],
        compiler_params=pltpu.CompilerParams(collective_id=0, has_side_effects=True, vmem_limit_bytes=40 * 1024 * 1024),
        name="layer",
    )(*[
        pltpu.with_memory_space_constraint(a, pltpu.HBM)
        for a in (
            table, batch_ids[0], tile_cols[0, 0], history[0], features[0], initial[0], grad_output[0], weight, tile_vals[0, 0],
        )
    ])
    new_hist, grad_x, grad_w = pl.pallas_call(
        hand_on,
        out_shape=shapes,
        in_specs=[vmem] * 3,
        out_specs=(hbm, hbm, hbm),
        scratch_shapes=[dma((6,))],
        compiler_params=pltpu.CompilerParams(vmem_limit_bytes=16 * 1024 * 1024),
        name="hand_on",
    )(*[pltpu.with_memory_space_constraint(a, pltpu.VMEM) for a in parts])
    return new_hist[None], grad_x[None], grad_w


def solution(mesh):
    return jax.shard_map(
        shards,
        mesh=mesh,
        in_specs=(
            P("dom", "batch", None),
            P("dom", "batch", None),
            P("dom", "batch", None),
            P(),
            P("dom", None, None),
            P("dom", "batch", None, None),
            P("dom", "batch", None, None),
            P("dom", "batch", None, None, None, None),
            P("dom", None, None),
        ),
        out_specs=(P("dom", None, None), P("dom", "batch", None), P()),
        check_vma=False,
    )
```

```python
import math

import jax
import jax.numpy as jnp
from jax import lax
from jax.experimental import pallas as pl
from jax.experimental.pallas import tpu as pltpu
from jax.sharding import PartitionSpec as P

ALPHA_MIX = 0.1
BETA_MIX = math.log(1.5)
X, Z, C, Y = 4, 16, 2, 4
N_DOM = X * Z * C
GROUP = X * Y * C
H = 256
TILE = 128
ROWS = 256
HIST = 4096
CAP = 8
K = 8
NB = 2 + N_DOM * CAP // TILE
PART = Y * ROWS
BASE = 8192
CHUNK = 512
FAR_PLANES = 9
BF = jnp.bfloat16
F32 = jnp.float32
I32 = jnp.int32


def coords():
    d = lax.axis_index("dom")
    return lax.div(d, Z * C), lax.rem(lax.div(d, C), Z), lax.rem(d, C), lax.axis_index("batch")


def dom_of(x, z, c):
    return (x * Z + z) * C + c


def each_dom_peer(fn, first=0, last=Z):
    x, z, c, _ = coords()

    def plane(zz, here, there, own):
        for i, (dx, back) in enumerate(((2, 0), (1, 2), (3, 1), (0, 3))):
            for j, dc in enumerate((1, 0)):
                if not (own and dx == 0 and dc == 0):
                    fn(dom_of(lax.rem(x + dx, X), zz, lax.rem(c + dc, C)), here * 8 + 2 * i + j, there * 8 + 2 * back + j)

    def body(k, carry):
        odd, half = lax.rem(k, 2), lax.div(k, 2)
        there = jnp.where(k == 0, 0, k + 2 * odd - 1)
        plane(lax.rem(z + Z // 2 + half * (1 - 2 * odd) - odd, Z), k, there, False)
        return carry

    lax.fori_loop(first, min(last, Z - 1), body, 0)
    if last == Z:
        plane(z, Z - 1, Z - 1, True)


def group_peers(skip_same_batch):
    x, z, c, b = coords()
    out = []
    for dx in (2, 1, 3, 0):
        for dy in (2, 1, 3, 0):
            for dc in (1, 0):
                if (dx, dy, dc) == (0, 0, 0) or (skip_same_batch and dy == 0):
                    continue
                qx, qy, qc = lax.rem(x + dx, X), lax.rem(b + dy, Y), lax.rem(c + dc, C)
                out.append(((qx * Y + qy) * C + qc, {"dom": dom_of(qx, z, qc), "batch": qy}))
    return out


def z_peers():
    x, z, c, _ = coords()
    return [{"dom": dom_of(x, lax.rem(z + i, Z), c)} for i in (8, 7, 9, 6, 10, 5, 11, 4, 12, 3, 13, 2, 14, 1, 15)]


def remote(src, dst, send, recv, device):
    return pltpu.make_async_remote_copy(src_ref=src, dst_ref=dst, send_sem=send, recv_sem=recv, device_id=device)


def wait_bytes(like, sem):
    pltpu.make_async_copy(like, like, sem).wait()


def iota(shape, dim):
    return lax.broadcasted_iota(I32, shape, dim)


def ones_where(mask):
    return jnp.where(mask, 1.0, 0.0).astype(BF)


def mm(a, b, dims=((1,), (0,))):
    return lax.dot_general(a, b, (dims, ((), ())), preferred_element_type=F32)


def kernel(
    tab_h, ids_h, cols_h, hist_h, feat_h, init_h, gout_h, w_h, tiles_h,
    nh_o, gx_o, gw_o,
    tab, ids, cols, hist, feat, init, gout, w, tiles,
    req, wreq, ntab, mixed, sbuf, rbuf, nsend, nrow, adj, adj_far, adj_near, place, base, live,
    outs, gsend, grecv, zsend, zrecv, asend, arecv,
    in_sem, req_s, req_r, nreq_s, nreq_r, row_s, row_r, nrow_s, nrow_r, rs_s, rs_r, z_s, z_r, ag_s, ag_r, y_s, y_r,
):
    x, z, c, b = coords()
    me = lax.axis_index("dom")
    pairs = [
        (tab_h, tab), (ids_h, ids), (cols_h, cols), (hist_h, hist), (feat_h, feat),
        (init_h, init), (gout_h, gout), (w_h, w), (tiles_h, tiles),
    ]
    loads = [pltpu.make_async_copy(src, dst, in_sem.at[i]) for i, (src, dst) in enumerate(pairs)]
    loads[0].start()
    barrier = pltpu.get_barrier_semaphore()
    each_dom_peer(lambda p, here, there: pl.semaphore_signal(barrier, inc=1, device_id={"dom": p}))
    others = group_peers(True)
    for _, device in others:
        pl.semaphore_signal(barrier, inc=1, device_id=device)
    for load in loads[1:]:
        load.start()

    loads[0].wait()
    req[...] = (tab[0:1, :] + 1) * BASE + (tab[1:2, :] + 1)
    wreq[N_DOM - 1] = jnp.zeros((1, N_DOM), I32)
    right, left = lax.rem(me + 1, N_DOM), lax.rem(me + N_DOM - 1, N_DOM)
    pl.semaphore_wait(barrier, N_DOM - 1 + len(others))
    near_req = [remote(tab, ntab.at[i], nreq_s.at[i], nreq_r.at[i], {"dom": p}) for i, p in enumerate((right, left))]
    each_dom_peer(lambda p, here, there: remote(req, wreq.at[there], req_s, req_r, {"dom": p}).start())
    for copy in near_req:
        copy.start()

    loads[1].wait()

    def place_chunk(i, carry):
        rows = iota((CHUNK, ROWS), 0) + i * CHUNK
        for q in range(Y):
            place[pl.ds(pl.multiple_of(i * CHUNK, CHUNK), CHUNK), pl.ds(q * ROWS, ROWS)] = ones_where(rows == ids[q : q + 1, :])
        return carry

    lax.fori_loop(0, HIST // CHUNK, place_chunk, 0)
    loads[3].wait()

    wait_bytes(wreq.at[pl.ds(0, N_DOM - 1)], req_r)
    for copy in near_req:
        copy.wait_recv()

    lane_me = iota((1, N_DOM), 1) == me

    def column(v):
        return jnp.sum(jnp.where(lane_me, v.astype(F32), 0.0), axis=1, keepdims=True)

    asked = wreq[...].reshape(N_DOM, N_DOM)
    one = column(lax.shift_right_logical(asked, 13) - 1)
    two = column(jnp.bitwise_and(asked, BASE - 1) - 1)
    cut = FAR_PLANES * X * C
    near_want = [column(tab[...]), column(ntab[0]), column(ntab[1]), jnp.full((8, 1), -1.0, F32)]
    wanted = jnp.concatenate([one[:cut], two[:cut], one[cut:], two[cut:], *near_want], axis=0).astype(I32)
    n_ask = 2 * N_DOM + 32
    block = jnp.where((wanted & 255) == iota((n_ask, 256), 1), (wanted >> 8).astype(F32), -1.0).astype(BF)
    def part(first, last):
        hot = jnp.concatenate([jnp.where(block[first:last] == BF(i), BF(1), BF(0)) for i in range(HIST // 256)], axis=1)
        return mm(hot, hist[...])

    def send_rows(rows, start, count, first, last):
        for i in range(2):
            for j in range(2):
                mixed[j, pl.ds(2 * start + i, count, 2), :] = rows[i * count : (i + 1) * count, j * TILE : (j + 1) * TILE]
        lines = slice(2 * start, 2 * (start + count))
        both = jnp.concatenate([mixed[0, lines, :], mixed[1, lines, :]], axis=1)
        sbuf[start : start + count] = both.astype(BF).reshape(count, 2, H)
        each_dom_peer(
            lambda p, here, there: remote(sbuf.at[here], rbuf.at[me], row_s, row_r, {"dom": p}).start(), first, last
        )

    rbuf[pl.ds(me, 1)] = jnp.zeros((1, 2, H), BF)
    send_rows(part(0, 2 * cut), 0, cut, 0, FAR_PLANES)
    got = part(2 * cut, n_ask)
    send_rows(got, cut, N_DOM - cut, FAR_PLANES, Z)
    n0 = 2 * (N_DOM - cut)
    nsend[0] = got[n0 + 16 : n0 + 24, :].astype(BF)
    nsend[1] = got[n0 + 8 : n0 + 16, :].astype(BF)
    near_row = [remote(nsend.at[i], nrow.at[i], nrow_s.at[i], nrow_r.at[i], {"dom": p}) for i, p in enumerate((right, left))]
    for copy in near_row:
        copy.start()

    own_rows = got[n0 : n0 + 8, :]
    for i in (2, 8):
        loads[i].wait()
    for r in range(2):
        for col in range(NB):
            at, found = jnp.int32(0), jnp.int32(1 if col == r else 0)
            for k in range(1, K if col != r else 1):
                same = cols[r, k] == col
                at, found = jnp.where(same, k, at), jnp.where(same, 1, found)
            tile = tiles[r, at]
            if col != r:
                tile = jnp.where(jnp.full((TILE, TILE), found, I32) > 0, tile.astype(F32), 0.0).astype(BF)
            adj[r * TILE : (r + 1) * TILE, col * TILE : (col + 1) * TILE] = tile
    shape = (N_DOM * CAP, 2 * N_DOM)
    p_row, p_col = iota(shape, 0), iota(shape, 1)
    slot = lax.rem(p_row, CAP)
    spread = ones_where(p_col == jnp.where(slot < 2, p_row // CAP * 2 + slot, -1))
    adj_far[...] = mm(adj[:, 2 * TILE :], spread).astype(BF)
    shape = (N_DOM * CAP, 32)
    p_row, p_col = iota(shape, 0), iota(shape, 1)
    who, slot = p_col // 8, lax.rem(p_col, 8)
    owner = jnp.where(who == 0, me, jnp.where(who == 1, left, right))
    spread = ones_where((p_row == owner * CAP + slot) & (who < 3) & ((who == 0) | (slot >= 2)))
    adj_near[...] = mm(adj[:, 2 * TILE :], spread).astype(BF)
    mine = jnp.sum(jnp.where(iota((Y, ROWS), 0) == b, (ids[...] >= 0).astype(F32), 0.0), axis=0, keepdims=True)
    live_col = jnp.sum(jnp.where(iota((ROWS, ROWS), 0) == iota((ROWS, ROWS), 1), mine, 0.0), axis=1, keepdims=True)
    live[...] = jnp.broadcast_to(live_col, (ROWS, H))
    loads[4].wait()
    loads[5].wait()
    masked = jnp.where(live[...] > 0, feat[...].astype(F32), 0.0).astype(BF)
    base[...] = (1.0 - ALPHA_MIX) * mm(adj[:, 0 : 2 * TILE], masked) + ALPHA_MIX * init[...].astype(F32)

    def clear_chunk(i, carry):
        rows = pl.ds(pl.multiple_of(i * CHUNK, CHUNK), CHUNK)
        hit = jnp.max(place[rows, :].astype(F32), axis=1, keepdims=True)
        nh_o[rows, :] = jnp.where(hit > 0, 0.0, hist[rows, :].astype(F32)).astype(BF)
        return carry

    lax.fori_loop(0, HIST // CHUNK, clear_chunk, 0)
    for i in (6, 7):
        loads[i].wait()

    for copy in near_row:
        copy.wait_recv()
    wait_bytes(rbuf.at[pl.ds(0, N_DOM - 1)], row_r)

    near = jnp.concatenate([own_rows, nrow[0].astype(F32), nrow[1].astype(F32), jnp.zeros((8, H), F32)], axis=0).astype(BF)

    halo = mm(adj_far[...], rbuf[...].reshape(2 * N_DOM, H)) + mm(adj_near[...], near)
    support = base[...] + (1.0 - ALPHA_MIX) * halo
    support_low = support.astype(BF)
    pre_act = (1.0 - BETA_MIX) * support + BETA_MIX * mm(support_low, w[...])
    sig = jax.nn.sigmoid(pre_act)
    slope = gout[...].astype(F32) * sig * (1.0 + pre_act * (1.0 - sig))
    grad_pre = jnp.where(live[...] > 0, slope, 0.0)
    grad_low = grad_pre.astype(BF)
    grad_w = mm(support_low, grad_low, ((0,), (0,)))

    gsend[...] = grad_w.astype(BF).reshape(GROUP, H // GROUP, H)
    slice_me = (x * Y + b) * C + c
    peers = group_peers(False)
    for slot_q, device in peers:
        remote(gsend.at[slot_q], grecv.at[slice_me], rs_s, rs_r, device).start()
    outs[pl.ds(b, 1)] = (pre_act * sig).astype(BF).reshape(1, ROWS, H)
    grecv[pl.ds(slice_me, 1)] = gsend[pl.ds(slice_me, 1)]

    grad_sup = (1.0 - BETA_MIX) * grad_pre + BETA_MIX * mm(grad_low, w[...], ((1,), (1,)))
    grad_agg = ((1.0 - ALPHA_MIX) * grad_sup).astype(BF)
    grad_x = mm(adj[:, 0 : 2 * TILE], grad_agg, ((0,), (0,)))
    gx_o[...] = jnp.where(live[...] > 0, grad_x, 0.0).astype(BF)

    wait_bytes(grecv.at[pl.ds(0, GROUP - 1)], rs_r)
    zsend[...] = jnp.sum(grecv[...].astype(F32), axis=0).astype(BF)
    for device in z_peers():
        remote(zsend, zrecv.at[z], z_s, z_r, device).start()
    zrecv[pl.ds(z, 1)] = zsend[...].reshape(1, H // GROUP, H)

    y_right, y_left = {"batch": lax.rem(b + 1, Y)}, {"batch": lax.rem(b + Y - 1, Y)}
    ring = [remote(outs.at[b], outs.at[b], y_s.at[i], y_r.at[i], p) for i, p in enumerate((y_right, y_left))]
    for copy in ring:
        copy.start()

    def scatter(q):
        lanes = pl.ds(pl.multiple_of(q * ROWS, ROWS), ROWS)
        for i in range(HIST // CHUNK):
            rows = pl.ds(i * CHUNK, CHUNK)
            nh_o[rows, :] = (nh_o[rows, :].astype(F32) + mm(place[rows, lanes], outs[q])).astype(BF)

    scatter(b)
    half = ROWS // 2
    before, after = lax.rem(b + Y - 1, Y), lax.rem(b + 1, Y)
    on = [
        remote(outs.at[before, pl.ds(0, half)], outs.at[before, pl.ds(0, half)], y_s.at[2], y_r.at[2], y_right),
        remote(outs.at[after, pl.ds(half, half)], outs.at[after, pl.ds(half, half)], y_s.at[3], y_r.at[3], y_left),
    ]
    ring[0].wait_recv()
    on[0].start()
    ring[1].wait_recv()
    on[1].start()
    scatter(before)
    wait_bytes(zrecv.at[pl.ds(0, Z - 1)], z_r)
    scale = BETA_MIX / (N_DOM * Y)
    asend[...] = (scale * jnp.sum(zrecv[...].astype(F32), axis=0)).astype(BF)
    for _, device in peers:
        remote(asend, arecv.at[slice_me], ag_s, ag_r, device).start()
    arecv[pl.ds(slice_me, 1)] = asend[...].reshape(1, H // GROUP, H)
    scatter(after)
    for copy in on:
        copy.wait_recv()
    scatter(lax.rem(b + 2, Y))

    for copy in near_req + near_row + ring + on:
        copy.wait_send()
    wait_bytes(wreq.at[pl.ds(0, N_DOM - 1)], req_s)
    wait_bytes(rbuf.at[pl.ds(0, N_DOM - 1)], row_s)
    wait_bytes(grecv.at[pl.ds(0, GROUP - 1)], rs_s)
    wait_bytes(zrecv.at[pl.ds(0, Z - 1)], z_s)
    wait_bytes(arecv.at[pl.ds(0, GROUP - 1)], ag_s)
    wait_bytes(arecv.at[pl.ds(0, GROUP - 1)], ag_r)
    gw_o[...] = arecv[...].astype(F32).reshape(H, H)


def hand_on(nh_i, gx_i, gw_i, nh_o, gx_o, gw_o, sem):
    step = HIST // 4
    parts = [(gw_i, gw_o), (gx_i, gx_o)]
    parts += [(nh_i.at[pl.ds(i * step, step)], nh_o.at[pl.ds(i * step, step)]) for i in range(4)]
    copies = [pltpu.make_async_copy(src, dst, sem.at[i]) for i, (src, dst) in enumerate(parts)]
    for copy in copies:
        copy.start()
    for copy in copies:
        copy.wait()


def shards(features, initial, grad_output, weight, history, halo_table, tile_cols, tile_vals, batch_ids):
    hbm = pl.BlockSpec(memory_space=pl.ANY)
    vmem = pl.BlockSpec(memory_space=pltpu.VMEM)
    v = pltpu.VMEM
    dma = pltpu.SemaphoreType.DMA
    table = jnp.transpose(halo_table[0, 0])
    shapes = (
        jax.ShapeDtypeStruct((HIST, H), BF),
        jax.ShapeDtypeStruct((ROWS, H), BF),
        jax.ShapeDtypeStruct((H, H), F32),
    )
    piece = H // GROUP
    parts = pl.pallas_call(
        kernel,
        out_shape=(v((HIST, H), BF), v((ROWS, H), BF), v((H, H), F32)),
        in_specs=[hbm] * 9,
        out_specs=(vmem, vmem, vmem),
        scratch_shapes=[
            v((CAP, N_DOM), I32), v((Y, ROWS), I32), pltpu.SMEM((2, K), I32), v((HIST, H), BF), v((ROWS, H), BF),
            v((ROWS, H), BF), v((ROWS, H), BF), v((H, H), BF), v((2, K, TILE, TILE), BF),
            v((1, N_DOM), I32), v((N_DOM, 1, N_DOM), I32), v((2, CAP, N_DOM), I32),
            v((2, 2 * N_DOM, TILE), F32), v((N_DOM, 2, H), BF), v((N_DOM, 2, H), BF), v((2, CAP, H), BF), v((2, CAP, H), BF),
            v((ROWS, NB * TILE), BF), v((ROWS, 2 * N_DOM), BF), v((ROWS, 32), BF), v((HIST, PART), BF),
            v((ROWS, H), F32), v((ROWS, H), F32),
            v((Y, ROWS, H), BF), v((GROUP, piece, H), BF), v((GROUP, piece, H), BF), v((piece, H), BF),
            v((Z, piece, H), BF), v((piece, H), BF), v((GROUP, piece, H), BF),
            dma((9,)), dma(()), dma(()), dma((2,)), dma((2,)), dma(()), dma(()), dma((2,)), dma((2,)),
            dma(()), dma(()), dma(()), dma(()), dma(()), dma(()), dma((4,)), dma((4,)),
        ],
        compiler_params=pltpu.CompilerParams(collective_id=0, has_side_effects=True, vmem_limit_bytes=40 * 1024 * 1024),
        name="layer",
    )(*[
        pltpu.with_memory_space_constraint(a, pltpu.HBM)
        for a in (
            table, batch_ids[0], tile_cols[0, 0], history[0], features[0], initial[0], grad_output[0], weight, tile_vals[0, 0],
        )
    ])
    new_hist, grad_x, grad_w = pl.pallas_call(
        hand_on,
        out_shape=shapes,
        in_specs=[vmem] * 3,
        out_specs=(hbm, hbm, hbm),
        scratch_shapes=[dma((6,))],
        compiler_params=pltpu.CompilerParams(vmem_limit_bytes=16 * 1024 * 1024),
        name="hand_on",
    )(*[pltpu.with_memory_space_constraint(a, pltpu.VMEM) for a in parts])
    return new_hist[None], grad_x[None], grad_w


def solution(mesh):
    return jax.shard_map(
        shards,
        mesh=mesh,
        in_specs=(
            P("dom", "batch", None),
            P("dom", "batch", None),
            P("dom", "batch", None),
            P(),
            P("dom", None, None),
            P("dom", "batch", None, None),
            P("dom", "batch", None, None),
            P("dom", "batch", None, None, None, None),
            P("dom", None, None),
        ),
        out_specs=(P("dom", None, None), P("dom", "batch", None), P()),
        check_vma=False,
    )
```
